32 devices in a mesh: row: 4 (over y, x), blk: 8 (over z, core).
Axes of the slice: x: 2, y: 2, z: 4, core: 2. Of those that a mesh axis runs over, the one named last changes fastest.
Arguments:
- cells: bfloat16 [8192, 768], P(('row', 'blk')), may hold values from -12 to 12
- tile_rows: int32 [384], P(('row', 'blk')), may hold values from 0 to 1, as said below
- tile_cols: int32 [384], P(('row', 'blk')), may hold values from 0 to 5, as said below
- tile_count: int32 [32], P(('row', 'blk')), may hold values from 6 to 12, as said below
- halo_blocks: int32 [32], P(('row', 'blk')), may hold values from 0 to 1, as said below
- tile_vals: bfloat16 [384, 128, 128], P(('row', 'blk')), may hold values from -0.375 to 0.375
- pool_ids: int32 [8192], P(('row', 'blk')), may hold values from 0 to 15, as said below
- w_msg: bfloat16 [768, 768], replicated, may hold values from -0.21875 to 0.21875
- w_query: bfloat16 [768, 768], replicated, may hold values from -1 to 2
- cotangent: bfloat16 [8192, 768], P(('row', 'blk')), may hold values from -6 to 6
Outputs:
- passed: bfloat16 [8192, 768], P(('row', 'blk'))
- attended: bfloat16 [8192, 768], P(('row', 'blk'))
- grad_cells: bfloat16 [8192, 768], P(('row', 'blk'))
The draws below stay inside these ranges and needn't reach their ends.
Inputs may be any that keep to these rules, and one draw needn't show every extreme that they name: `tile_rows`: slot i of a partition's 12 slots, for i < 2, has row i. `tile_cols`: slot i of a partition, for i < 6, has column i; later slots have columns below 2. `tile_count`: slots of a partition at or beyond its count are unused. `halo_blocks`: distinct within one partition. `pool_ids`: every supernode of a partition has at least one of its cells; the first two cells of a partition lie in supernodes 0 and 1.
All inputs are finite; a program needn't handle non-finite values.
Results may differ from the reference program's by a relative error of at most 0.04.
The reference program's roundings to bfloat16 on the way count: a program that leaves them out, or rounds other values in their place, can miss the bound.
Values may be sent and summed in bfloat16 or wider, within the bound.
A program may use at most 64 MiB of HBM per device.

```python
import math
import jax
import jax.numpy as jnp
from jax import lax

D = 768
HEADS = 12
HEAD = 64
BLOCK = 128
NB = 2
HB = 1
SN_DEV = 16
GRID = 32
EXT = 6
TILES = 12
CELL_DEV = 256
CELLS = 8192
TILE_ALL = 384
N_ROW = 4
N_BLK = 8


def draw_cells(key, part):
    base = jnp.clip(jax.random.normal(key, (CELLS, D), jnp.float32), -6.0, 6.0)
    return base.astype(jnp.bfloat16)


def draw_tile_rows(key, part):
    slot_index = jnp.arange(TILES, dtype=jnp.int32)[None, :]
    random_rows = jax.random.randint(key, (GRID, TILES), 0, NB, dtype=jnp.int32)
    return jnp.where(slot_index < NB, slot_index, random_rows).reshape(-1)


def draw_tile_cols(key, part):
    slot_index = jnp.arange(TILES, dtype=jnp.int32)[None, :]
    random_cols = jax.random.randint(jax.random.fold_in(key, 11), (GRID, TILES), 0, NB, dtype=jnp.int32)
    return jnp.where(slot_index < NB + 4 * HB, slot_index, random_cols).reshape(-1)


def draw_tile_count(key, part):
    heavy_mask = jax.random.randint(key, (GRID,), 0, 8, dtype=jnp.int32) == 0
    counts = jnp.where(heavy_mask, TILES, NB + 4 * HB).astype(jnp.int32)
    return counts.at[0].set(TILES).at[1].set(NB + 4 * HB)


def draw_halo_blocks(key, part):
    scores_int = jax.random.randint(key, (GRID, NB), 0, 1 << 20, dtype=jnp.int32) * NB + jnp.arange(NB, dtype=jnp.int32)[None, :]
    ordering = jnp.argsort(scores_int, axis=1, stable=True)
    return ordering[:, :HB].astype(jnp.int32).reshape(-1)


def draw_pool_ids(key, part):
    first_key, second_key = jax.random.split(key)
    labels = jax.random.randint(first_key, (GRID, CELL_DEV), 0, SN_DEV, dtype=jnp.int32)
    ranking = jax.random.randint(second_key, (GRID, CELL_DEV - 2), 0, 1 << 16, dtype=jnp.int32) * CELL_DEV + jnp.arange(CELL_DEV - 2, dtype=jnp.int32)[None, :]
    ordering = jnp.argsort(ranking, axis=1, stable=True)[:, :SN_DEV].astype(jnp.int32) + 2
    device_rows = jnp.broadcast_to(jnp.arange(GRID, dtype=jnp.int32)[:, None], (GRID, SN_DEV))
    labels = labels.at[device_rows, ordering].set(jnp.broadcast_to(jnp.arange(SN_DEV, dtype=jnp.int32)[None, :], (GRID, SN_DEV)))
    labels = labels.at[:, 0].set(0).at[:, 1].set(1)
    return labels.reshape(-1)


def draw_w_query(key, part):
    first_key = jax.random.fold_in(key, 0)
    noise = jnp.clip(jax.random.normal(first_key, (D, D), jnp.float32) * (2.0 / math.sqrt(D)), -1.0, 1.0)
    return noise.astype(jnp.bfloat16)


def block_levels(stream_key, extent, cuts, low, largest):
    def one(position, blocks):
        steps = jax.random.uniform(jax.random.fold_in(jax.random.fold_in(stream_key, 6), position), (blocks,), jnp.float32, low / len(cuts), largest / len(cuts))
        return jnp.repeat(jnp.exp(steps), extent[position] // blocks).reshape((-1,) + (1,) * (len(extent) - position - 1))

    loudness = one(*cuts[0])
    for cut in cuts[1:]:
        loudness = loudness * one(*cut)
    return loudness


def centred(rng, dims, deviation, bound, shards=(), held_as=jnp.bfloat16):
    values = deviation * jax.random.normal(rng, dims, jnp.float32)
    if shards:
        values = values * block_levels(rng, dims, shards, -0.22, 0.18)
    return jnp.clip(values, -bound, bound).astype(held_as)


def setup_inputs(seed: int = 0) -> dict:
    seeds = jax.random.split(jax.random.key(seed), 11)
    cells = draw_cells(jax.random.fold_in(seeds[10], 71), 0)
    tile_rows = draw_tile_rows(jax.random.fold_in(seeds[10], 71), 0)
    tile_cols = draw_tile_cols(jax.random.fold_in(seeds[10], 71), 0)
    tile_count = draw_tile_count(jax.random.fold_in(seeds[10], 71), 0)
    halo_blocks = draw_halo_blocks(jax.random.fold_in(seeds[10], 71), 0)
    tile_vals = centred(seeds[5], (TILE_ALL, BLOCK, BLOCK), (2 * BLOCK) ** -0.5, 0.375, ((0, 32),))
    pool_ids = draw_pool_ids(jax.random.fold_in(seeds[10], 71), 0)
    w_msg = centred(seeds[7], (D, D), D ** -0.5, 0.21875)
    w_query = draw_w_query(jax.random.fold_in(seeds[10], 71), 0)
    cotangent = centred(seeds[9], (CELLS, D), 1.0, 6.0, ((0, 32),))
    return dict(cells=cells, tile_rows=tile_rows, tile_cols=tile_cols, tile_count=tile_count, halo_blocks=halo_blocks, tile_vals=tile_vals, pool_ids=pool_ids, w_msg=w_msg, w_query=w_query, cotangent=cotangent)


def silu_slope(values):
    sigma = jax.nn.sigmoid(values)
    return sigma * (1.0 + values * (1.0 - sigma))

def shift_grid(grid, row_step, col_step):
    padded = jnp.pad(grid, ((1, 1), (1, 1)) + ((0, 0),) * (grid.ndim - 2))
    return padded[1 - row_step:1 - row_step + N_ROW, 1 - col_step:1 - col_step + N_BLK]

def pick_rows(source, indices):
    return source[indices]

def reference(cells, tile_rows, tile_cols, tile_count, halo_blocks, tile_vals, pool_ids, w_msg, w_query, cotangent):
    grid_count = N_ROW * N_BLK
    blocks = cells.reshape(grid_count, NB, BLOCK, D)
    halo_index = halo_blocks.reshape(grid_count, HB).astype(jnp.int32)
    boundary = jax.vmap(pick_rows)(blocks, halo_index)
    bound_grid = boundary.reshape(N_ROW, N_BLK, HB, BLOCK, D)
    extended = jnp.concatenate([blocks.reshape(N_ROW, N_BLK, NB, BLOCK, D), shift_grid(bound_grid, 1, 0), shift_grid(bound_grid, -1, 0), shift_grid(bound_grid, 0, 1), shift_grid(bound_grid, 0, -1)], axis=2).reshape(grid_count, EXT, BLOCK, D)
    rows_dev = tile_rows.reshape(grid_count, TILES)
    cols_dev = tile_cols.reshape(grid_count, TILES)
    vals_dev = tile_vals.reshape(grid_count, TILES, BLOCK, BLOCK)
    live_mask = (jnp.arange(TILES, dtype=jnp.int32)[None, :] < tile_count[:, None]).astype(jnp.float32)

    def forward_tiles(inputs):
        ext_dev, row_ids, col_ids, tile_block, alive_mask = inputs
        picked = ext_dev[col_ids].astype(jnp.float32)
        product = jnp.einsum('tab,tbd->tad', tile_block.astype(jnp.float32), picked) * alive_mask[:, None, None]
        choose = (row_ids[None, :] == jnp.arange(NB, dtype=jnp.int32)[:, None]).astype(jnp.float32)
        return jnp.einsum('nt,tad->nad', choose, product)
    message = lax.map(forward_tiles, (extended, rows_dev, cols_dev, vals_dev, live_mask)).astype(jnp.bfloat16).reshape(CELLS, D)
    hidden = jnp.dot(message, w_msg, preferred_element_type=jnp.float32)
    passed = (cells.astype(jnp.float32) + jax.nn.silu(hidden)).astype(jnp.bfloat16)
    member = (pool_ids.reshape(grid_count, 1, CELL_DEV) == jnp.arange(SN_DEV, dtype=jnp.int32)[None, :, None]).astype(jnp.float32)
    counts = lax.optimization_barrier(jnp.sum(member, axis=2))
    pooled = jnp.einsum('dsc,dcf->dsf', member, passed.reshape(grid_count, CELL_DEV, D).astype(jnp.float32))
    supern = (pooled / jnp.sqrt(counts)[:, :, None]).astype(jnp.bfloat16)
    query_proj = jnp.dot(passed, w_query, preferred_element_type=jnp.float32).astype(jnp.bfloat16)
    score_scale = HEAD ** (-0.5)

    def attend(inputs):
        query_row, keys_row, cot_row = inputs
        queries = query_row.reshape(-1, HEADS, HEAD).astype(jnp.float32)
        key_rows = keys_row.reshape(-1, HEADS, HEAD).astype(jnp.float32)
        grads = cot_row.reshape(-1, HEADS, HEAD).astype(jnp.float32)
        scores = jnp.einsum('qhe,khe->hqk', queries, key_rows) * score_scale
        weights = jnp.exp(scores - lax.optimization_barrier(jnp.max(scores, axis=2, keepdims=True)))
        weights = weights / lax.optimization_barrier(jnp.sum(weights, axis=2, keepdims=True))
        rounded = weights.astype(jnp.bfloat16).astype(jnp.float32)
        values_sum = jnp.einsum('hqk,khe->qhe', rounded, key_rows)
        centre = lax.optimization_barrier(jnp.sum(grads * values_sum, axis=2))
        slope = jnp.einsum('qhe,khe->hqk', grads, key_rows)
        dscore = (weights * (slope - centre.T[:, :, None]) * score_scale).astype(jnp.bfloat16).astype(jnp.float32)
        dquery = jnp.einsum('hqk,khe->qhe', dscore, key_rows).astype(jnp.bfloat16)
        dkey = jnp.einsum('hqk,qhe->khe', dscore, queries) + jnp.einsum('hqk,qhe->khe', rounded, grads)
        return (values_sum.astype(jnp.bfloat16).reshape(-1, D), dquery.reshape(-1, D), dkey.reshape(-1, D))
    attended, dquery, dkey = lax.map(attend, (query_proj.reshape(N_ROW, -1, D), supern.reshape(N_ROW, -1, D), cotangent.reshape(N_ROW, -1, D)))
    attended = attended.reshape(CELLS, D)
    dquery = dquery.reshape(CELLS, D)
    key_grad = dkey.reshape(grid_count, SN_DEV, D)
    pool_grad = (key_grad / jnp.sqrt(counts)[:, :, None]).astype(jnp.bfloat16)
    spread = jnp.einsum('dsc,dsf->dcf', member, pool_grad.astype(jnp.float32)).reshape(CELLS, D)
    through = (cotangent.astype(jnp.float32) + jnp.dot(dquery, w_query.T, preferred_element_type=jnp.float32) + spread).astype(jnp.bfloat16)
    dhidden = (through.astype(jnp.float32) * silu_slope(hidden)).astype(jnp.bfloat16)
    dmessage = jnp.dot(dhidden, w_msg.T, preferred_element_type=jnp.float32).astype(jnp.bfloat16).reshape(grid_count, NB, BLOCK, D)

    def backward_tiles(inputs):
        grad_dev, row_ids, col_ids, tile_block, alive_mask = inputs
        picked = grad_dev[row_ids].astype(jnp.float32)
        product = jnp.einsum('tab,tad->tbd', tile_block.astype(jnp.float32), picked) * alive_mask[:, None, None]
        choose = (col_ids[None, :] == jnp.arange(EXT, dtype=jnp.int32)[:, None]).astype(jnp.float32)
        return jnp.einsum('et,tbd->ebd', choose, product)
    ext_grad = lax.map(backward_tiles, (dmessage, rows_dev, cols_dev, vals_dev, live_mask)).reshape(N_ROW, N_BLK, EXT, BLOCK, D)
    own_grad = ext_grad[:, :, :NB].reshape(grid_count, NB, BLOCK, D)
    from_up = ext_grad[:, :, NB:NB + HB]
    from_down = ext_grad[:, :, NB + HB:NB + 2 * HB]
    from_left = ext_grad[:, :, NB + 2 * HB:NB + 3 * HB]
    from_right = ext_grad[:, :, NB + 3 * HB:NB + 4 * HB]
    returned = shift_grid(from_up, -1, 0) + shift_grid(from_down, 1, 0) + shift_grid(from_left, 0, -1) + shift_grid(from_right, 0, 1)
    placing = (halo_index[:, None, :] == jnp.arange(NB, dtype=jnp.int32)[None, :, None]).astype(jnp.float32)
    summed = through.astype(jnp.float32).reshape(grid_count, NB, BLOCK, D) + own_grad + jnp.einsum('dnh,dhbf->dnbf', placing, returned.reshape(grid_count, HB, BLOCK, D), precision=lax.Precision.HIGHEST)
    grad_cells = summed.astype(jnp.bfloat16).reshape(CELLS, D)
    return (passed, attended, grad_cells)
```

```python
import functools

import jax
import jax.numpy as jnp
from jax import lax
from jax.experimental import pallas as pl
from jax.experimental.pallas import tpu as pltpu
from jax.sharding import PartitionSpec as P

D = 768
HEAD = 64
BLOCK = 128
NB = 2
SN_DEV = 16
EXT = 6
TILES = 12
CELL_DEV = 256
PAIR = 2 * HEAD
CHUNK = 256
CHUNKS = D // CHUNK
LOG2E = 1.4426950408889634
BF = jnp.bfloat16
F32 = jnp.float32
MESH = pl.DeviceIdType.MESH


def dot(a, b):
    return jnp.dot(a, b, preferred_element_type=F32)


def dot_nt(a, b):
    return lax.dot_general(a, b, (((1,), (1,)), ((), ())), preferred_element_type=F32)


def cols(j, width=CHUNK):
    return slice(j * width, (j + 1) * width)


def kernel(
    n_row, n_blk,
    cells, rows, colsr, count, halo, tiles, pool, w_msg, w_query, cot,
    passed_o, att_o, grad_o,
    ext, bnd, tv, wm, wq, cv, adj, adj_lo, adj_t, wm_t, wq_t, msg, hid, sig, pas, qry, keys,
    att, dqr, kg, kgr, gs, gr, own, out, dh, base, dm, via,
    lc, ld, st, hs, hr, ks, kr, ps, pr, ss, sr, vr, vs,
):
    r = lax.axis_index("row")
    c = lax.axis_index("blk")
    nk = SN_DEV * n_blk

    loads = [
        pltpu.make_async_copy(tiles, tv, ld.at[1]),
        pltpu.make_async_copy(w_msg, wm, ld.at[2]),
        pltpu.make_async_copy(w_query, wq, ld.at[3]),
        pltpu.make_async_copy(cot, cv, ld.at[4]),
    ]
    cell_loads = [
        pltpu.make_async_copy(cells.at[:, pl.ds(j * CHUNK, CHUNK)], ext.at[j, pl.ds(0, CELL_DEV)], lc.at[j])
        for j in range(CHUNKS)
    ]
    for load in cell_loads + loads:
        load.start()

    barrier = pltpu.get_barrier_semaphore()
    for off in range(1, n_blk):
        pl.semaphore_signal(
            barrier, inc=1, device_id=(r, lax.rem(c + off, n_blk)), device_id_type=MESH
        )

    has_up, has_down = r > 0, r < n_row - 1
    has_left, has_right = c > 0, c < n_blk - 1
    up, down = jnp.maximum(r - 1, 0), jnp.minimum(r + 1, n_row - 1)
    left, right = jnp.maximum(c - 1, 0), jnp.minimum(c + 1, n_blk - 1)

    relay = n_row == 4
    if relay:
        middle = jnp.where(lax.rem(c, 2) == 0, 0, n_row - 1)
        hands_on = r == middle
        diagonal = (r == 2, r == 1)
        for off in range(1, n_row):
            pl.semaphore_signal(
                barrier, inc=1, device_id=(lax.rem(r + off, n_row), c), device_id_type=MESH
            )
        greeted = (n_blk - 1) + (n_row - 1)
    else:
        @pl.when(has_up)
        def _():
            pl.semaphore_signal(barrier, inc=1, device_id=(up, c), device_id_type=MESH)

        @pl.when(has_down)
        def _():
            pl.semaphore_signal(barrier, inc=1, device_id=(down, c), device_id_type=MESH)

        greeted = (n_blk - 1) + has_up.astype(jnp.int32) + has_down.astype(jnp.int32)

    sides = (
        (has_up, (up, c)),
        (has_down, (down, c)),
        (has_left, (r, left)),
        (has_right, (r, right)),
    )

    def halo_send(j, s):
        there = NB + (s ^ 1)
        return pltpu.make_async_remote_copy(
            src_ref=bnd.at[j],
            dst_ref=ext.at[j, pl.ds(there * BLOCK, BLOCK)],
            send_sem=hs.at[j, s],
            recv_sem=hr.at[j, s ^ 1],
            device_id=sides[s][1],
            device_id_type=MESH,
        )

    def straight(s):
        if relay and s < 2:
            return sides[s][0] & jnp.logical_not(diagonal[s])
        return sides[s][0]

    def to_middle(phase, part, sem, j, s):
        return pltpu.make_async_remote_copy(
            src_ref=part,
            dst_ref=via.at[phase, j, s],
            send_sem=sem.at[j, s],
            recv_sem=vr.at[phase, j, s],
            device_id=(middle, c),
            device_id_type=MESH,
        )

    def from_middle(phase, j, s):
        if phase == 0:
            there = ext.at[j, pl.ds((NB + (s ^ 1)) * BLOCK, BLOCK)]
            sem = hr.at[j, s ^ 1]
        else:
            there = gr.at[j, s ^ 1]
            sem = sr.at[j, s ^ 1]
        return pltpu.make_async_remote_copy(
            src_ref=via.at[phase, j, s],
            dst_ref=there,
            send_sem=vs.at[phase, j, s],
            recv_sem=sem,
            device_id=((1, 2)[s], c),
            device_id_type=MESH,
        )

    def hand_on(phase, j):
        if relay:
            for s in (0, 1):
                @pl.when(hands_on)
                def _():
                    to_middle(phase, bnd.at[j], hs, j, s).wait_recv()
                    from_middle(phase, j, s).start()

    def halo_recv(j, s):
        return pltpu.make_async_remote_copy(
            src_ref=bnd.at[j],
            dst_ref=ext.at[j, pl.ds((NB + s) * BLOCK, BLOCK)],
            send_sem=hs.at[j, s],
            recv_sem=hr.at[j, s],
            device_id=sides[s][1],
            device_id_type=MESH,
        )

    def key_copy(j, off):
        return pltpu.make_async_remote_copy(
            src_ref=keys.at[j, pl.ds(pl.multiple_of(c * SN_DEV, SN_DEV), SN_DEV)],
            dst_ref=keys.at[j, pl.ds(pl.multiple_of(c * SN_DEV, SN_DEV), SN_DEV)],
            send_sem=ks.at[j, off],
            recv_sem=kr.at[j, off],
            device_id=(r, lax.rem(c + off, n_blk)),
            device_id_type=MESH,
        )

    def key_recv(j, off):
        source = lax.rem(c + n_blk - off, n_blk)
        part = keys.at[j, pl.ds(pl.multiple_of(source * SN_DEV, SN_DEV), SN_DEV)]
        return pltpu.make_async_remote_copy(
            src_ref=part, dst_ref=part, send_sem=ks.at[j, off], recv_sem=kr.at[j, off],
            device_id=(r, source), device_id_type=MESH,
        )

    def part_copy(j, off):
        peer = lax.rem(c + off, n_blk)
        return pltpu.make_async_remote_copy(
            src_ref=kg.at[j, pl.ds(pl.multiple_of(peer * SN_DEV, SN_DEV), SN_DEV)],
            dst_ref=kgr.at[j, off],
            send_sem=ps.at[j, off],
            recv_sem=pr.at[j, off],
            device_id=(r, peer),
            device_id_type=MESH,
        )

    def grad_send(j, s):
        return pltpu.make_async_remote_copy(
            src_ref=gs.at[j, s],
            dst_ref=gr.at[j, s ^ 1],
            send_sem=ss.at[j, s],
            recv_sem=sr.at[j, s ^ 1],
            device_id=sides[s][1],
            device_id_type=MESH,
        )

    def grad_recv(j, s):
        return pltpu.make_async_remote_copy(
            src_ref=gs.at[j, s],
            dst_ref=gr.at[j, s],
            send_sem=ss.at[j, s],
            recv_sem=sr.at[j, s],
            device_id=sides[s][1],
            device_id_type=MESH,
        )

    second = (halo[0] == 1).astype(F32)
    for j in range(CHUNKS):
        cell_loads[j].wait()
        bnd[j] = (
            ext[j, :BLOCK].astype(F32) * (1.0 - second)
            + ext[j, BLOCK:CELL_DEV].astype(F32) * second
        ).astype(BF)
    pl.semaphore_wait(barrier, greeted)
    if relay:
        for j in range(CHUNKS):
            for s in (0, 1):
                @pl.when(diagonal[s])
                def _():
                    to_middle(0, bnd.at[j], hs, j, s).start()
    for j in range(CHUNKS):
        for s in range(4):
            @pl.when(straight(s))
            def _():
                halo_send(j, s).start()

            @pl.when(jnp.logical_not(sides[s][0]))
            def _():
                ext[j, (NB + s) * BLOCK : (NB + s + 1) * BLOCK] = jnp.zeros((BLOCK, CHUNK), BF)
                gr[j, s] = jnp.zeros((BLOCK, CHUNK), BF)

    loads[0].wait()
    live = count[0]
    for i in range(NB):
        at = slice(i * BLOCK, (i + 1) * BLOCK)
        for k in range(NB):
            total = tv[k].astype(F32) if i == k else jnp.zeros((BLOCK, BLOCK), F32)
            for s in range(EXT, TILES):
                use = (live > s) & (rows[s] == i) & (colsr[s] == k)
                total = total + tv[s].astype(F32) * use.astype(F32)
            high = total.astype(BF)
            adj[at, k * BLOCK : (k + 1) * BLOCK] = high
            adj_lo[at, k * BLOCK : (k + 1) * BLOCK] = (total - high.astype(F32)).astype(BF)
        for k in range(NB, EXT):
            use = (rows[k] == i).astype(F32)
            adj[at, k * BLOCK : (k + 1) * BLOCK] = (tv[k].astype(F32) * use).astype(BF)
    for k in range(CHUNKS):
        adj_t[cols(k), :] = adj[:, cols(k)].T
    for j in range(CHUNKS):
        own_cells = ext[j, :CELL_DEV]
        msg[:, cols(j)] = dot(adj[:, :CELL_DEV], own_cells) + dot(adj_lo[...], own_cells)
    ids = pool[...]
    member = (ids == lax.broadcasted_iota(jnp.int32, (SN_DEV, CELL_DEV), 0)).astype(F32)
    member_b = member.astype(BF)
    wide = (ids == lax.broadcasted_iota(jnp.int32, (PAIR, CELL_DEV), 0)).astype(F32)
    member_t = wide.T.astype(BF)
    root = jnp.sqrt(jnp.sum(member, axis=1, keepdims=True))
    loads[1].wait()
    loads[2].wait()
    for j in range(CHUNKS):
        hand_on(0, j)
        for k in range(CHUNKS):
            wm_t[cols(k), cols(j)] = wm[cols(j), cols(k)].T
            wq_t[cols(k), cols(j)] = wq[cols(j), cols(k)].T
    loads[3].wait()

    for j in range(CHUNKS):
        for s in (2, 3):
            @pl.when(sides[s][0])
            def _():
                halo_recv(j, s).wait_recv()
        msg[:, cols(j)] += dot(adj[:, 2 * CELL_DEV :], ext[j, 2 * CELL_DEV :])
    for j in range(CHUNKS):
        for s in (0, 1):
            @pl.when(sides[s][0])
            def _():
                halo_recv(j, s).wait_recv()
        part = (
            msg[:, cols(j)]
            + dot(adj[:, CELL_DEV : 2 * CELL_DEV], ext[j, CELL_DEV : 2 * CELL_DEV])
        ).astype(BF)
        if j == CHUNKS - 1:
            break
        for k in range(CHUNKS):
            term = dot(part, wm[cols(j), cols(k)])
            hid[:, cols(k)] = term if j == 0 else hid[:, cols(k)] + term
    mine = pl.ds(pl.multiple_of(c * SN_DEV, SN_DEV), SN_DEV)
    for j in range(CHUNKS):
        hidden = hid[:, cols(j)] + dot(part, wm[cols(CHUNKS - 1), cols(j)])
        sigma = jax.nn.sigmoid(hidden)
        hid[:, cols(j)] = hidden
        sig[:, cols(j)] = sigma
        passed = (ext[j, :CELL_DEV].astype(F32) + hidden * sigma).astype(BF)
        pas[:, cols(j)] = passed
        keys[j, mine] = (dot(member_b, passed) / root).astype(BF)
        for off in range(1, n_blk):
            key_copy(j, off).start()
    stores = [pltpu.make_async_copy(pas, passed_o, st.at[0])]
    stores[0].start()
    for j in range(CHUNKS):
        qry[:, cols(j)] = dot(pas[...], wq[:, cols(j)]).astype(BF)

    lane = lax.broadcasted_iota(jnp.int32, (1, PAIR), 1)
    even_f = (lane < HEAD).astype(F32)
    even, odd = even_f.astype(BF), (1.0 - even_f).astype(BF)
    scale = HEAD ** (-0.5)
    per = CHUNK // PAIR
    for t in range(D // PAIR):
        at = cols(t, PAIR)
        group, inner = t // per, cols(t % per, PAIR)
        if t % per == 0:
            for off in range(1, n_blk):
                key_recv(group, off).wait_recv()
        kp = keys[group, :, inner]
        k2 = jnp.concatenate([kp * even, kp * odd], axis=0)
        qp, cp = qry[:, at], cv[:, at]
        scores = dot_nt(k2, qp).reshape(2, nk, CELL_DEV)
        slope = dot_nt(k2, cp).reshape(2, nk, CELL_DEV)
        top = jnp.max(scores, axis=1, keepdims=True)
        probs = jnp.exp2((scores - top) * (scale * LOG2E))
        probs = probs * (1.0 / jnp.sum(probs, axis=1, keepdims=True))
        rounded = probs.astype(BF)
        centre = jnp.sum(rounded.astype(F32) * slope, axis=1, keepdims=True)
        dscore = (probs * (slope - centre) * scale).astype(BF)
        rounded = rounded.reshape(2 * nk, CELL_DEV)
        dscore = dscore.reshape(2 * nk, CELL_DEV)
        both = dot(dscore, qp) + dot(rounded, cp)
        kg[group, :, inner] = jnp.where(lane < HEAD, both[:nk], both[nk:]).astype(BF)
        if t % per == per - 1:
            for off in range(1, n_blk):
                part_copy(group, off).start()
        att[:, at] = dot(rounded.T, k2).astype(BF)
        dqr[:, at] = dot(dscore.T, k2).astype(BF)
    stores.append(pltpu.make_async_copy(att, att_o, st.at[1]))
    stores[1].start()
    for j in range(CHUNKS):
        base[:, cols(j)] = cv[:, cols(j)].astype(F32) + dot(dqr[...], wq_t[:, cols(j)])
        sigma = sig[:, cols(j)]
        sig[:, cols(j)] = sigma * (1.0 + hid[:, cols(j)] * (1.0 - sigma))
    for j in range(CHUNKS):
        total = kg[j, mine].astype(F32)
        for off in range(1, n_blk):
            part_copy(j, off).wait_recv()
            total = total + kgr[j, off].astype(F32)
        spread = dot(member_t[:, :SN_DEV], (total / root).astype(BF))
        through = (base[:, cols(j)] + spread).astype(BF).astype(F32)
        base[:, cols(j)] = through
        dh[:, cols(j)] = (through * sig[:, cols(j)]).astype(BF)
    for j in range(CHUNKS):
        dmsg = dot(dh[...], wm_t[:, cols(j)]).astype(BF)
        dm[:, cols(j)] = dmsg
        back = dot(adj_t[CELL_DEV:, :], dmsg)
        for s in range(4):
            gs[j, s] = back[s * BLOCK : (s + 1) * BLOCK].astype(BF)
        if relay:
            for s in (0, 1):
                @pl.when(diagonal[s])
                def _():
                    to_middle(1, gs.at[j, s], ss, j, s).start()
        for s in range(4):
            @pl.when(straight(s))
            def _():
                grad_send(j, s).start()
    for j in range(CHUNKS):
        hand_on(1, j)
        own[:, cols(j)] = base[:, cols(j)] + dot(adj_t[:CELL_DEV, :], dm[:, cols(j)])
    for j in range(CHUNKS):
        for s in (2, 3, 0, 1):
            @pl.when(sides[s][0])
            def _():
                grad_recv(j, s).wait_recv()
        returned = (
            gr[j, 0].astype(F32) + gr[j, 1].astype(F32)
            + gr[j, 2].astype(F32) + gr[j, 3].astype(F32)
        )
        out[:BLOCK, cols(j)] = (own[:BLOCK, cols(j)] + returned * (1.0 - second)).astype(BF)
        out[BLOCK:, cols(j)] = (own[BLOCK:, cols(j)] + returned * second).astype(BF)
    stores.append(pltpu.make_async_copy(out, grad_o, st.at[2]))
    stores[2].start()

    for s in range(4):
        @pl.when(straight(s))
        def _():
            for j in range(CHUNKS):
                halo_send(j, s).wait_send()
                grad_send(j, s).wait_send()
    if relay:
        for s in (0, 1):
            @pl.when(diagonal[s])
            def _():
                for j in range(CHUNKS):
                    to_middle(0, bnd.at[j], hs, j, s).wait_send()
                    to_middle(1, gs.at[j, s], ss, j, s).wait_send()

            @pl.when(hands_on)
            def _():
                for j in range(CHUNKS):
                    from_middle(0, j, s).wait_send()
                    from_middle(1, j, s).wait_send()
    for off in range(1, n_blk):
        for j in range(CHUNKS):
            key_copy(j, off).wait_send()
            part_copy(j, off).wait_send()
    for store in stores:
        store.wait()


def hand_over(a, b, c, a_o, b_o, c_o, sems):
    half = CELL_DEV // 2
    copies = [
        pltpu.make_async_copy(
            source.at[pl.ds(k * half, half)], target.at[pl.ds(k * half, half)], sems.at[i, k]
        )
        for i, (source, target) in enumerate(((a, a_o), (b, b_o), (c, c_o)))
        for k in range(2)
    ]
    for copy in copies:
        copy.start()
    for copy in copies:
        copy.wait()


def body(n_row, n_blk, cells, tile_rows, tile_cols, tile_count, halo_blocks, tile_vals, pool_ids,
         w_msg, w_query, cotangent):
    any_spec = pl.BlockSpec(memory_space=pl.ANY)
    smem = pl.BlockSpec(memory_space=pltpu.SMEM)
    vmem = pl.BlockSpec(memory_space=pltpu.VMEM)
    nk = SN_DEV * n_blk
    whole = (CELL_DEV, D)
    sem = pltpu.SemaphoreType.DMA
    results = pl.pallas_call(
        functools.partial(kernel, n_row, n_blk),
        out_shape=[jax.ShapeDtypeStruct(whole, BF)] * 3,
        in_specs=[any_spec, smem, smem, smem, smem, any_spec, vmem, any_spec, any_spec, any_spec],
        out_specs=[any_spec] * 3,
        scratch_shapes=[
            pltpu.VMEM((CHUNKS, EXT * BLOCK, CHUNK), BF),
            pltpu.VMEM((CHUNKS, BLOCK, CHUNK), BF),
            pltpu.VMEM((TILES, BLOCK, BLOCK), BF),
            pltpu.VMEM((D, D), BF),
            pltpu.VMEM((D, D), BF),
            pltpu.VMEM(whole, BF),
            pltpu.VMEM((CELL_DEV, EXT * BLOCK), BF),
            pltpu.VMEM((CELL_DEV, CELL_DEV), BF),
            pltpu.VMEM((EXT * BLOCK, CELL_DEV), BF),
            pltpu.VMEM((D, D), BF),
            pltpu.VMEM((D, D), BF),
            pltpu.VMEM(whole, F32),
            pltpu.VMEM(whole, F32),
            pltpu.VMEM(whole, F32),
            pltpu.VMEM(whole, BF),
            pltpu.VMEM(whole, BF),
            pltpu.VMEM((CHUNKS, nk, CHUNK), BF),
            pltpu.VMEM(whole, BF),
            pltpu.VMEM(whole, BF),
            pltpu.VMEM((CHUNKS, nk, CHUNK), BF),
            pltpu.VMEM((CHUNKS, n_blk, SN_DEV, CHUNK), BF),
            pltpu.VMEM((CHUNKS, 4, BLOCK, CHUNK), BF),
            pltpu.VMEM((CHUNKS, 4, BLOCK, CHUNK), BF),
            pltpu.VMEM(whole, F32),
            pltpu.VMEM(whole, BF),
            pltpu.VMEM(whole, BF),
            pltpu.VMEM(whole, F32),
            pltpu.VMEM(whole, BF),
            pltpu.VMEM((2, CHUNKS, 2, BLOCK, CHUNK), BF),
            sem((CHUNKS,)), sem((5,)), sem((3,)), sem((CHUNKS, 4)), sem((CHUNKS, 4)),
            sem((CHUNKS, n_blk)), sem((CHUNKS, n_blk)), sem((CHUNKS, n_blk)), sem((CHUNKS, n_blk)),
            sem((CHUNKS, 4)), sem((CHUNKS, 4)), sem((2, CHUNKS, 2)), sem((2, CHUNKS, 2)),
        ],
        compiler_params=pltpu.CompilerParams(
            collective_id=0, has_side_effects=True, vmem_limit_bytes=63 * 1024 * 1024
        ),
    )(cells, tile_rows, tile_cols, tile_count, halo_blocks, tile_vals,
      pool_ids.reshape(1, CELL_DEV), w_msg, w_query, cotangent)
    return pl.pallas_call(
        hand_over,
        out_shape=[jax.ShapeDtypeStruct(whole, BF)] * 3,
        in_specs=[any_spec] * 3,
        out_specs=[any_spec] * 3,
        scratch_shapes=[sem((3, 2))],
        compiler_params=pltpu.CompilerParams(vmem_limit_bytes=63 * 1024 * 1024),
    )(*results)


def solution(mesh):
    both = P(("row", "blk"))
    flat = P(("row", "blk"), None)
    return jax.shard_map(
        functools.partial(body, mesh.shape["row"], mesh.shape["blk"]),
        mesh=mesh,
        in_specs=(flat, both, both, both, both, P(("row", "blk"), None, None), both, P(), P(), flat),
        out_specs=(flat, flat, flat),
        check_vma=False,
    )
```

```python
import functools

import jax
import jax.numpy as jnp
from jax import lax
from jax.experimental import pallas as pl
from jax.experimental.pallas import tpu as pltpu
from jax.sharding import PartitionSpec as P

D = 768
HEAD = 64
BLOCK = 128
NB = 2
SN_DEV = 16
EXT = 6
TILES = 12
CELL_DEV = 256
PAIR = 2 * HEAD
CHUNK = 256
CHUNKS = D // CHUNK
LOG2E = 1.4426950408889634
BF = jnp.bfloat16
F32 = jnp.float32
MESH = pl.DeviceIdType.MESH


def dot(a, b):
    return jnp.dot(a, b, preferred_element_type=F32)


def dot_nt(a, b):
    return lax.dot_general(a, b, (((1,), (1,)), ((), ())), preferred_element_type=F32)


def cols(j, width=CHUNK):
    return slice(j * width, (j + 1) * width)


def kernel(
    n_row, n_blk,
    cells, rows_h, cols_h, count, halo, tiles, pool_h, w_msg, w_query, cot,
    pas, att, out,
    ext, bnd, tv, wm, wq, cv, adj, adj_lo, adj_t, wm_t, wq_t, msg, hid, sig, qry, keys,
    dqr, kg, kgr, gs, gr, own, dh, base, dm, via, cv_t, sc, sl, pb, ds,
    lc, ld, hs, hr, ks, kr, ps, pr, ss, sr, vr, vs, rows, colsr, pool, li,
):
    r = lax.axis_index("row")
    c = lax.axis_index("blk")
    nk = SN_DEV * n_blk

    loads = [
        pltpu.make_async_copy(tiles, tv, ld.at[1]),
        pltpu.make_async_copy(w_msg, wm, ld.at[2]),
        pltpu.make_async_copy(w_query, wq, ld.at[3]),
        pltpu.make_async_copy(cot, cv, ld.at[4]),
    ]
    cell_loads = [
        pltpu.make_async_copy(cells.at[:, pl.ds(j * CHUNK, CHUNK)], ext.at[j, pl.ds(0, CELL_DEV)], lc.at[j])
        for j in range(CHUNKS)
    ]
    ints = [
        pltpu.make_async_copy(rows_h, rows, li.at[0]),
        pltpu.make_async_copy(cols_h, colsr, li.at[1]),
        pltpu.make_async_copy(pool_h, pool, li.at[2]),
    ]
    for load in cell_loads + ints + loads:
        load.start()

    barrier = pltpu.get_barrier_semaphore()
    for off in range(1, n_blk):
        pl.semaphore_signal(
            barrier, inc=1, device_id=(r, lax.rem(c + off, n_blk)), device_id_type=MESH
        )

    has_up, has_down = r > 0, r < n_row - 1
    has_left, has_right = c > 0, c < n_blk - 1
    up, down = jnp.maximum(r - 1, 0), jnp.minimum(r + 1, n_row - 1)
    left, right = jnp.maximum(c - 1, 0), jnp.minimum(c + 1, n_blk - 1)

    relay = n_row == 4
    if relay:
        middle = jnp.where(lax.rem(c, 2) == 0, 0, n_row - 1)
        hands_on = r == middle
        diagonal = (r == 2, r == 1)
        for off in range(1, n_row):
            pl.semaphore_signal(
                barrier, inc=1, device_id=(lax.rem(r + off, n_row), c), device_id_type=MESH
            )
        greeted = (n_blk - 1) + (n_row - 1)
    else:
        @pl.when(has_up)
        def _():
            pl.semaphore_signal(barrier, inc=1, device_id=(up, c), device_id_type=MESH)

        @pl.when(has_down)
        def _():
            pl.semaphore_signal(barrier, inc=1, device_id=(down, c), device_id_type=MESH)

        greeted = (n_blk - 1) + has_up.astype(jnp.int32) + has_down.astype(jnp.int32)

    sides = (
        (has_up, (up, c)),
        (has_down, (down, c)),
        (has_left, (r, left)),
        (has_right, (r, right)),
    )

    def halo_send(j, s):
        there = NB + (s ^ 1)
        return pltpu.make_async_remote_copy(
            src_ref=bnd.at[j],
            dst_ref=ext.at[j, pl.ds(there * BLOCK, BLOCK)],
            send_sem=hs.at[j, s],
            recv_sem=hr.at[j, s ^ 1],
            device_id=sides[s][1],
            device_id_type=MESH,
        )

    def straight(s):
        if relay and s < 2:
            return sides[s][0] & jnp.logical_not(diagonal[s])
        return sides[s][0]

    def to_middle(phase, part, sem, j, s):
        return pltpu.make_async_remote_copy(
            src_ref=part,
            dst_ref=via.at[phase, j, s],
            send_sem=sem.at[j, s],
            recv_sem=vr.at[phase, j, s],
            device_id=(middle, c),
            device_id_type=MESH,
        )

    def from_middle(phase, j, s):
        if phase == 0:
            there = ext.at[j, pl.ds((NB + (s ^ 1)) * BLOCK, BLOCK)]
            sem = hr.at[j, s ^ 1]
        else:
            there = gr.at[j, s ^ 1]
            sem = sr.at[j, s ^ 1]
        return pltpu.make_async_remote_copy(
            src_ref=via.at[phase, j, s],
            dst_ref=there,
            send_sem=vs.at[phase, j, s],
            recv_sem=sem,
            device_id=((1, 2)[s], c),
            device_id_type=MESH,
        )

    def hand_on(phase, j):
        if relay:
            for s in (0, 1):
                @pl.when(hands_on)
                def _():
                    to_middle(phase, bnd.at[j], hs, j, s).wait_recv()
                    from_middle(phase, j, s).start()

    def halo_recv(j, s):
        return pltpu.make_async_remote_copy(
            src_ref=bnd.at[j],
            dst_ref=ext.at[j, pl.ds((NB + s) * BLOCK, BLOCK)],
            send_sem=hs.at[j, s],
            recv_sem=hr.at[j, s],
            device_id=sides[s][1],
            device_id_type=MESH,
        )

    def key_copy(j, off):
        return pltpu.make_async_remote_copy(
            src_ref=keys.at[j, pl.ds(pl.multiple_of(c * SN_DEV, SN_DEV), SN_DEV)],
            dst_ref=keys.at[j, pl.ds(pl.multiple_of(c * SN_DEV, SN_DEV), SN_DEV)],
            send_sem=ks.at[j, off],
            recv_sem=kr.at[j, off],
            device_id=(r, lax.rem(c + off, n_blk)),
            device_id_type=MESH,
        )

    def key_recv(j, off):
        source = lax.rem(c + n_blk - off, n_blk)
        part = keys.at[j, pl.ds(pl.multiple_of(source * SN_DEV, SN_DEV), SN_DEV)]
        return pltpu.make_async_remote_copy(
            src_ref=part, dst_ref=part, send_sem=ks.at[j, off], recv_sem=kr.at[j, off],
            device_id=(r, source), device_id_type=MESH,
        )

    def part_copy(j, off):
        peer = lax.rem(c + off, n_blk)
        return pltpu.make_async_remote_copy(
            src_ref=kg.at[j, pl.ds(pl.multiple_of(peer * SN_DEV, SN_DEV), SN_DEV)],
            dst_ref=kgr.at[j, off],
            send_sem=ps.at[j, off],
            recv_sem=pr.at[j, off],
            device_id=(r, peer),
            device_id_type=MESH,
        )

    def grad_send(j, s):
        return pltpu.make_async_remote_copy(
            src_ref=gs.at[j, s],
            dst_ref=gr.at[j, s ^ 1],
            send_sem=ss.at[j, s],
            recv_sem=sr.at[j, s ^ 1],
            device_id=sides[s][1],
            device_id_type=MESH,
        )

    def grad_recv(j, s):
        return pltpu.make_async_remote_copy(
            src_ref=gs.at[j, s],
            dst_ref=gr.at[j, s],
            send_sem=ss.at[j, s],
            recv_sem=sr.at[j, s],
            device_id=sides[s][1],
            device_id_type=MESH,
        )

    second = (halo[0] == 1).astype(F32)
    for j in range(CHUNKS):
        cell_loads[j].wait()
        bnd[j] = (
            ext[j, :BLOCK].astype(F32) * (1.0 - second)
            + ext[j, BLOCK:CELL_DEV].astype(F32) * second
        ).astype(BF)
    pl.semaphore_wait(barrier, greeted)
    if relay:
        for j in range(CHUNKS):
            for s in (0, 1):
                @pl.when(diagonal[s])
                def _():
                    to_middle(0, bnd.at[j], hs, j, s).start()
    for j in range(CHUNKS):
        for s in range(4):
            @pl.when(straight(s))
            def _():
                halo_send(j, s).start()

            @pl.when(jnp.logical_not(sides[s][0]))
            def _():
                ext[j, (NB + s) * BLOCK : (NB + s + 1) * BLOCK] = jnp.zeros((BLOCK, CHUNK), BF)
                gr[j, s] = jnp.zeros((BLOCK, CHUNK), BF)

    loads[0].wait()
    for load in ints:
        load.wait()
    live = count[0]
    for i in range(NB):
        at = slice(i * BLOCK, (i + 1) * BLOCK)
        for k in range(NB):
            total = tv[k].astype(F32) if i == k else jnp.zeros((BLOCK, BLOCK), F32)
            for s in range(EXT, TILES):
                use = (live > s) & (rows[s] == i) & (colsr[s] == k)
                total = total + tv[s].astype(F32) * use.astype(F32)
            high = total.astype(BF)
            adj[at, k * BLOCK : (k + 1) * BLOCK] = high
            adj_lo[at, k * BLOCK : (k + 1) * BLOCK] = (total - high.astype(F32)).astype(BF)
        for k in range(NB, EXT):
            use = (rows[k] == i).astype(F32)
            adj[at, k * BLOCK : (k + 1) * BLOCK] = (tv[k].astype(F32) * use).astype(BF)
    for k in range(CHUNKS):
        adj_t[cols(k), :] = adj[:, cols(k)].T
    for j in range(CHUNKS):
        own_cells = ext[j, :CELL_DEV]
        msg[:, cols(j)] = dot(adj[:, :CELL_DEV], own_cells) + dot(adj_lo[...], own_cells)
    ids = pool[...]
    member = (ids == lax.broadcasted_iota(jnp.int32, (SN_DEV, CELL_DEV), 0)).astype(F32)
    member_b = member.astype(BF)
    wide = (ids == lax.broadcasted_iota(jnp.int32, (PAIR, CELL_DEV), 0)).astype(F32)
    member_t = wide.T.astype(BF)
    root = jnp.sqrt(jnp.sum(member, axis=1, keepdims=True))
    loads[1].wait()
    loads[2].wait()
    for j in range(CHUNKS):
        hand_on(0, j)
        for k in range(CHUNKS):
            wm_t[cols(k), cols(j)] = wm[cols(j), cols(k)].T
            wq_t[cols(k), cols(j)] = wq[cols(j), cols(k)].T
    loads[3].wait()
    for j in range(CHUNKS):
        cv_t[cols(j), :] = cv[:, cols(j)].T

    for j in range(CHUNKS):
        for s in (2, 3):
            @pl.when(sides[s][0])
            def _():
                halo_recv(j, s).wait_recv()
        msg[:, cols(j)] += dot(adj[:, 2 * CELL_DEV :], ext[j, 2 * CELL_DEV :])
    for j in range(CHUNKS):
        for s in (0, 1):
            @pl.when(sides[s][0])
            def _():
                halo_recv(j, s).wait_recv()
        part = (
            msg[:, cols(j)]
            + dot(adj[:, CELL_DEV : 2 * CELL_DEV], ext[j, CELL_DEV : 2 * CELL_DEV])
        ).astype(BF)
        if j == CHUNKS - 1:
            break
        for k in range(CHUNKS):
            term = dot(part, wm[cols(j), cols(k)])
            hid[:, cols(k)] = term if j == 0 else hid[:, cols(k)] + term
    mine = pl.ds(pl.multiple_of(c * SN_DEV, SN_DEV), SN_DEV)
    for j in range(CHUNKS):
        hid[:, cols(j)] += dot(part, wm[cols(CHUNKS - 1), cols(j)])
        for first in range(0, CELL_DEV, 64):
            some = slice(first, first + 64)
            hidden = hid[some, cols(j)]
            sigma = jax.nn.sigmoid(hidden)
            sig[some, cols(j)] = sigma
            pas[some, cols(j)] = (ext[j, some].astype(F32) + hidden * sigma).astype(BF)
        passed = pas[:, cols(j)]
        keys[j, mine] = (dot(member_b, passed) / root).astype(BF)
        for off in range(1, n_blk):
            key_copy(j, off).start()
    for j in range(CHUNKS):
        qry[:, cols(j)] = dot(pas[...], wq[:, cols(j)]).astype(BF)

    lane = lax.broadcasted_iota(jnp.int32, (1, PAIR), 1)
    even_f = (lane < HEAD).astype(F32)
    even, odd = even_f.astype(BF), (1.0 - even_f).astype(BF)
    scale = HEAD ** (-0.5)
    line = lax.broadcasted_iota(jnp.int32, (PAIR, 1), 0)
    upper_f = (line < HEAD).astype(F32)
    upper, lower = upper_f.astype(BF), (1.0 - upper_f).astype(BF)
    per = CHUNK // PAIR
    for t in range(D // PAIR):
        at = cols(t, PAIR)
        group, inner = t // per, cols(t % per, PAIR)
        if t % per == 0:
            for off in range(1, n_blk):
                key_recv(group, off).wait_recv()
        kp = keys[group, :, inner]
        k2 = jnp.concatenate([kp * even, kp * odd], axis=0)
        kp_t = kp.T
        k2_t = jnp.concatenate([kp_t * upper, kp_t * lower], axis=1)
        qp, cp = qry[:, at], cv[:, at]
        w = t % 2
        sc[w] = dot_nt(k2, qp)
        sl[w] = dot(k2, cv_t[at, :])
        for h in range(2):
            head = slice(h * nk, (h + 1) * nk)
            for x in range(CELL_DEV // BLOCK):
                some = cols(x, BLOCK)
                scores = sc[w, head, some]
                top = jnp.max(scores, axis=0, keepdims=True)
                probs = jnp.exp2((scores - top) * (scale * LOG2E))
                probs = probs * (1.0 / jnp.sum(probs, axis=0, keepdims=True))
                rounded = probs.astype(BF)
                pb[w, head, some] = rounded
                slope = sl[w, head, some]
                centre = jnp.sum(rounded.astype(F32) * slope, axis=0, keepdims=True)
                ds[w, head, some] = (probs * (slope - centre) * scale).astype(BF)
        both = dot(ds[w], qp) + dot(pb[w], cp)
        kg[group, :, inner] = jnp.where(lane < HEAD, both[:nk], both[nk:]).astype(BF)
        if t % per == per - 1:
            for off in range(1, n_blk):
                part_copy(group, off).start()
        att[:, at] = dot(k2_t, pb[w]).astype(BF).T
        dqr[:, at] = dot(k2_t, ds[w]).astype(BF).T
    for j in range(CHUNKS):
        base[:, cols(j)] = cv[:, cols(j)].astype(F32) + dot(dqr[...], wq_t[:, cols(j)])
        sigma = sig[:, cols(j)]
        sig[:, cols(j)] = sigma * (1.0 + hid[:, cols(j)] * (1.0 - sigma))
    for j in range(CHUNKS):
        total = kg[j, mine].astype(F32)
        for off in range(1, n_blk):
            part_copy(j, off).wait_recv()
            total = total + kgr[j, off].astype(F32)
        spread = dot(member_t[:, :SN_DEV], (total / root).astype(BF))
        through = (base[:, cols(j)] + spread).astype(BF).astype(F32)
        base[:, cols(j)] = through
        dh[:, cols(j)] = (through * sig[:, cols(j)]).astype(BF)
    for j in range(CHUNKS):
        dmsg = dot(dh[...], wm_t[:, cols(j)]).astype(BF)
        dm[:, cols(j)] = dmsg
        back = dot(adj_t[CELL_DEV:, :], dmsg)
        for s in range(4):
            gs[j, s] = back[s * BLOCK : (s + 1) * BLOCK].astype(BF)
        if relay:
            for s in (0, 1):
                @pl.when(diagonal[s])
                def _():
                    to_middle(1, gs.at[j, s], ss, j, s).start()
        for s in range(4):
            @pl.when(straight(s))
            def _():
                grad_send(j, s).start()
    for j in range(CHUNKS):
        hand_on(1, j)
        own[:, cols(j)] = base[:, cols(j)] + dot(adj_t[:CELL_DEV, :], dm[:, cols(j)])
    for j in range(CHUNKS):
        for s in (2, 3, 0, 1):
            @pl.when(sides[s][0])
            def _():
                grad_recv(j, s).wait_recv()
        returned = (
            gr[j, 0].astype(F32) + gr[j, 1].astype(F32)
            + gr[j, 2].astype(F32) + gr[j, 3].astype(F32)
        )
        out[:BLOCK, cols(j)] = (own[:BLOCK, cols(j)] + returned * (1.0 - second)).astype(BF)
        out[BLOCK:, cols(j)] = (own[BLOCK:, cols(j)] + returned * second).astype(BF)

    for s in range(4):
        @pl.when(straight(s))
        def _():
            for j in range(CHUNKS):
                halo_send(j, s).wait_send()
                grad_send(j, s).wait_send()
    if relay:
        for s in (0, 1):
            @pl.when(diagonal[s])
            def _():
                for j in range(CHUNKS):
                    to_middle(0, bnd.at[j], hs, j, s).wait_send()
                    to_middle(1, gs.at[j, s], ss, j, s).wait_send()

            @pl.when(hands_on)
            def _():
                for j in range(CHUNKS):
                    from_middle(0, j, s).wait_send()
                    from_middle(1, j, s).wait_send()
    for off in range(1, n_blk):
        for j in range(CHUNKS):
            key_copy(j, off).wait_send()
            part_copy(j, off).wait_send()


def hand_over(a, b, c, a_o, b_o, c_o, sems):
    half = CELL_DEV // 2
    copies = [
        pltpu.make_async_copy(
            source.at[pl.ds(k * half, half)], target.at[pl.ds(k * half, half)], sems.at[i, k]
        )
        for i, (source, target) in enumerate(((a, a_o), (b, b_o), (c, c_o)))
        for k in range(2)
    ]
    for copy in copies:
        copy.start()
    for copy in copies:
        copy.wait()


def body(n_row, n_blk, cells, tile_rows, tile_cols, tile_count, halo_blocks, tile_vals, pool_ids,
         w_msg, w_query, cotangent):
    any_spec = pl.BlockSpec(memory_space=pl.ANY)
    smem = pl.BlockSpec(memory_space=pltpu.SMEM)
    hbm = pl.BlockSpec(memory_space=pltpu.HBM)
    nk = SN_DEV * n_blk
    whole = (CELL_DEV, D)
    sem = pltpu.SemaphoreType.DMA
    results = pl.pallas_call(
        functools.partial(kernel, n_row, n_blk),
        out_shape=[pltpu.VMEM(whole, BF)] * 3,
        in_specs=[hbm, hbm, hbm, smem, smem, hbm, hbm, hbm, hbm, hbm],
        out_specs=[pl.BlockSpec(memory_space=pltpu.VMEM)] * 3,
        scratch_shapes=[
            pltpu.VMEM((CHUNKS, EXT * BLOCK, CHUNK), BF),
            pltpu.VMEM((CHUNKS, BLOCK, CHUNK), BF),
            pltpu.VMEM((TILES, BLOCK, BLOCK), BF),
            pltpu.VMEM((D, D), BF),
            pltpu.VMEM((D, D), BF),
            pltpu.VMEM(whole, BF),
            pltpu.VMEM((CELL_DEV, EXT * BLOCK), BF),
            pltpu.VMEM((CELL_DEV, CELL_DEV), BF),
            pltpu.VMEM((EXT * BLOCK, CELL_DEV), BF),
            pltpu.VMEM((D, D), BF),
            pltpu.VMEM((D, D), BF),
            pltpu.VMEM(whole, F32),
            pltpu.VMEM(whole, F32),
            pltpu.VMEM(whole, F32),
            pltpu.VMEM(whole, BF),
            pltpu.VMEM((CHUNKS, nk, CHUNK), BF),
            pltpu.VMEM(whole, BF),
            pltpu.VMEM((CHUNKS, nk, CHUNK), BF),
            pltpu.VMEM((CHUNKS, n_blk, SN_DEV, CHUNK), BF),
            pltpu.VMEM((CHUNKS, 4, BLOCK, CHUNK), BF),
            pltpu.VMEM((CHUNKS, 4, BLOCK, CHUNK), BF),
            pltpu.VMEM(whole, F32),
            pltpu.VMEM(whole, BF),
            pltpu.VMEM(whole, F32),
            pltpu.VMEM(whole, BF),
            pltpu.VMEM((2, CHUNKS, 2, BLOCK, CHUNK), BF),
            pltpu.VMEM((D, CELL_DEV), BF),
            pltpu.VMEM((2, 2 * nk, CELL_DEV), F32),
            pltpu.VMEM((2, 2 * nk, CELL_DEV), F32),
            pltpu.VMEM((2, 2 * nk, CELL_DEV), BF),
            pltpu.VMEM((2, 2 * nk, CELL_DEV), BF),
            sem((CHUNKS,)), sem((5,)), sem((CHUNKS, 4)), sem((CHUNKS, 4)),
            sem((CHUNKS, n_blk)), sem((CHUNKS, n_blk)), sem((CHUNKS, n_blk)), sem((CHUNKS, n_blk)),
            sem((CHUNKS, 4)), sem((CHUNKS, 4)), sem((2, CHUNKS, 2)), sem((2, CHUNKS, 2)),
            pltpu.SMEM((TILES,), jnp.int32), pltpu.SMEM((TILES,), jnp.int32),
            pltpu.VMEM((1, CELL_DEV), jnp.int32), sem((3,)),
        ],
        compiler_params=pltpu.CompilerParams(
            collective_id=0, has_side_effects=True, vmem_limit_bytes=(62 * 1024 + 768) * 1024
        ),
    )(cells, tile_rows, tile_cols, tile_count, halo_blocks, tile_vals,
      pool_ids.reshape(1, CELL_DEV), w_msg, w_query, cotangent)
    return pl.pallas_call(
        hand_over,
        out_shape=[jax.ShapeDtypeStruct(whole, BF)] * 3,
        in_specs=[any_spec] * 3,
        out_specs=[hbm] * 3,
        scratch_shapes=[sem((3, 2))],
    )(*results)


def solution(mesh):
    both = P(("row", "blk"))
    flat = P(("row", "blk"), None)
    return jax.shard_map(
        functools.partial(body, mesh.shape["row"], mesh.shape["blk"]),
        mesh=mesh,
        in_specs=(flat, both, both, both, both, P(("row", "blk"), None, None), both, P(), P(), flat),
        out_specs=(flat, flat, flat),
        check_vma=False,
    )
```

```python
import functools

import jax
import jax.numpy as jnp
from jax import lax
from jax.experimental import pallas as pl
from jax.experimental.pallas import tpu as pltpu
from jax.sharding import PartitionSpec as P

D = 768
HEAD = 64
BLOCK = 128
NB = 2
SN_DEV = 16
EXT = 6
TILES = 12
CELL_DEV = 256
PAIR = 2 * HEAD
CHUNK = 256
CHUNKS = D // CHUNK
LOG2E = 1.4426950408889634
BF = jnp.bfloat16
F32 = jnp.float32
MESH = pl.DeviceIdType.MESH


def dot(a, b):
    return jnp.dot(a, b, preferred_element_type=F32)


def dot_nt(a, b):
    return lax.dot_general(a, b, (((1,), (1,)), ((), ())), preferred_element_type=F32)


def cols(j, width=CHUNK):
    return slice(j * width, (j + 1) * width)


def kernel(
    n_row, n_blk,
    cells, rows_h, cols_h, count, halo, tiles, pool_h, w_msg, w_query, cot,
    pas, att, out,
    ext, bnd, tv, wm, wq, cv, adj, adj_lo, adj_t, wm_t, wq_t, msg, hid, sig, qry, keys,
    dqr, kg, kgr, gs, gr, own, dh, base, dm, via, cv_t, sc, sl, pb, ds,
    lc, ld, hs, hr, ks, kr, ps, pr, ss, sr, vr, vs, rows, colsr, pool, li,
):
    r = lax.axis_index("row")
    c = lax.axis_index("blk")
    nk = SN_DEV * n_blk

    loads = [
        pltpu.make_async_copy(tiles, tv, ld.at[1]),
        pltpu.make_async_copy(w_msg, wm, ld.at[2]),
        pltpu.make_async_copy(w_query, wq, ld.at[3]),
        pltpu.make_async_copy(cot, cv, ld.at[4]),
    ]
    cell_loads = [
        pltpu.make_async_copy(cells.at[:, pl.ds(j * CHUNK, CHUNK)], ext.at[j, pl.ds(0, CELL_DEV)], lc.at[j])
        for j in range(CHUNKS)
    ]
    ints = [
        pltpu.make_async_copy(rows_h, rows, li.at[0]),
        pltpu.make_async_copy(cols_h, colsr, li.at[1]),
        pltpu.make_async_copy(pool_h, pool, li.at[2]),
    ]
    for load in cell_loads + ints + loads:
        load.start()

    barrier = pltpu.get_barrier_semaphore()
    for off in range(1, n_blk):
        pl.semaphore_signal(
            barrier, inc=1, device_id=(r, lax.rem(c + off, n_blk)), device_id_type=MESH
        )

    has_up, has_down = r > 0, r < n_row - 1
    has_left, has_right = c > 0, c < n_blk - 1
    up, down = jnp.maximum(r - 1, 0), jnp.minimum(r + 1, n_row - 1)
    left, right = jnp.maximum(c - 1, 0), jnp.minimum(c + 1, n_blk - 1)

    relay = n_row == 4
    if relay:
        middle = jnp.where(lax.rem(c, 2) == 0, 0, n_row - 1)
        hands_on = r == middle
        diagonal = (r == 2, r == 1)
        for off in range(1, n_row):
            pl.semaphore_signal(
                barrier, inc=1, device_id=(lax.rem(r + off, n_row), c), device_id_type=MESH
            )
        greeted = (n_blk - 1) + (n_row - 1)
    else:
        @pl.when(has_up)
        def _():
            pl.semaphore_signal(barrier, inc=1, device_id=(up, c), device_id_type=MESH)

        @pl.when(has_down)
        def _():
            pl.semaphore_signal(barrier, inc=1, device_id=(down, c), device_id_type=MESH)

        greeted = (n_blk - 1) + has_up.astype(jnp.int32) + has_down.astype(jnp.int32)

    sides = (
        (has_up, (up, c)),
        (has_down, (down, c)),
        (has_left, (r, left)),
        (has_right, (r, right)),
    )

    def halo_send(j, s):
        there = NB + (s ^ 1)
        return pltpu.make_async_remote_copy(
            src_ref=bnd.at[j],
            dst_ref=ext.at[j, pl.ds(there * BLOCK, BLOCK)],
            send_sem=hs.at[j, s],
            recv_sem=hr.at[j, s ^ 1],
            device_id=sides[s][1],
            device_id_type=MESH,
        )

    def straight(s):
        if relay and s < 2:
            return sides[s][0] & jnp.logical_not(diagonal[s])
        return sides[s][0]

    def to_middle(phase, part, sem, j, s):
        return pltpu.make_async_remote_copy(
            src_ref=part,
            dst_ref=via.at[phase, j, s],
            send_sem=sem.at[j, s],
            recv_sem=vr.at[phase, j, s],
            device_id=(middle, c),
            device_id_type=MESH,
        )

    def from_middle(phase, j, s):
        if phase == 0:
            there = ext.at[j, pl.ds((NB + (s ^ 1)) * BLOCK, BLOCK)]
            sem = hr.at[j, s ^ 1]
        else:
            there = gr.at[j, s ^ 1]
            sem = sr.at[j, s ^ 1]
        return pltpu.make_async_remote_copy(
            src_ref=via.at[phase, j, s],
            dst_ref=there,
            send_sem=vs.at[phase, j, s],
            recv_sem=sem,
            device_id=((1, 2)[s], c),
            device_id_type=MESH,
        )

    def hand_on(phase, j):
        if relay:
            for s in (0, 1):
                @pl.when(hands_on)
                def _():
                    to_middle(phase, bnd.at[j], hs, j, s).wait_recv()
                    from_middle(phase, j, s).start()

    def halo_recv(j, s):
        return pltpu.make_async_remote_copy(
            src_ref=bnd.at[j],
            dst_ref=ext.at[j, pl.ds((NB + s) * BLOCK, BLOCK)],
            send_sem=hs.at[j, s],
            recv_sem=hr.at[j, s],
            device_id=sides[s][1],
            device_id_type=MESH,
        )

    def key_copy(j, off):
        return pltpu.make_async_remote_copy(
            src_ref=keys.at[j, pl.ds(pl.multiple_of(c * SN_DEV, SN_DEV), SN_DEV)],
            dst_ref=keys.at[j, pl.ds(pl.multiple_of(c * SN_DEV, SN_DEV), SN_DEV)],
            send_sem=ks.at[j, off],
            recv_sem=kr.at[j, off],
            device_id=(r, lax.rem(c + off, n_blk)),
            device_id_type=MESH,
        )

    def key_recv(j, off):
        source = lax.rem(c + n_blk - off, n_blk)
        part = keys.at[j, pl.ds(pl.multiple_of(source * SN_DEV, SN_DEV), SN_DEV)]
        return pltpu.make_async_remote_copy(
            src_ref=part, dst_ref=part, send_sem=ks.at[j, off], recv_sem=kr.at[j, off],
            device_id=(r, source), device_id_type=MESH,
        )

    def part_copy(j, off):
        peer = lax.rem(c + off, n_blk)
        return pltpu.make_async_remote_copy(
            src_ref=kg.at[j, pl.ds(pl.multiple_of(peer * SN_DEV, SN_DEV), SN_DEV)],
            dst_ref=kgr.at[j, off],
            send_sem=ps.at[j, off],
            recv_sem=pr.at[j, off],
            device_id=(r, peer),
            device_id_type=MESH,
        )

    def grad_send(j, s):
        return pltpu.make_async_remote_copy(
            src_ref=gs.at[j, s],
            dst_ref=gr.at[j, s ^ 1],
            send_sem=ss.at[j, s],
            recv_sem=sr.at[j, s ^ 1],
            device_id=sides[s][1],
            device_id_type=MESH,
        )

    def grad_recv(j, s):
        return pltpu.make_async_remote_copy(
            src_ref=gs.at[j, s],
            dst_ref=gr.at[j, s],
            send_sem=ss.at[j, s],
            recv_sem=sr.at[j, s],
            device_id=sides[s][1],
            device_id_type=MESH,
        )

    second = (halo[0] == 1).astype(F32)
    for j in range(CHUNKS):
        cell_loads[j].wait()
        bnd[j] = (
            ext[j, :BLOCK].astype(F32) * (1.0 - second)
            + ext[j, BLOCK:CELL_DEV].astype(F32) * second
        ).astype(BF)
    pl.semaphore_wait(barrier, greeted)
    if relay:
        for j in range(CHUNKS):
            for s in (0, 1):
                @pl.when(diagonal[s])
                def _():
                    to_middle(0, bnd.at[j], hs, j, s).start()
    for j in range(CHUNKS):
        for s in range(4):
            @pl.when(straight(s))
            def _():
                halo_send(j, s).start()

            @pl.when(jnp.logical_not(sides[s][0]))
            def _():
                ext[j, (NB + s) * BLOCK : (NB + s + 1) * BLOCK] = jnp.zeros((BLOCK, CHUNK), BF)
                gr[j, s] = jnp.zeros((BLOCK, CHUNK), BF)

    loads[0].wait()
    for load in ints:
        load.wait()
    live = count[0]
    for i in range(NB):
        at = slice(i * BLOCK, (i + 1) * BLOCK)
        for k in range(NB):
            total = tv[k].astype(F32) if i == k else jnp.zeros((BLOCK, BLOCK), F32)
            for s in range(EXT, TILES):
                use = (live > s) & (rows[s] == i) & (colsr[s] == k)
                total = total + tv[s].astype(F32) * use.astype(F32)
            high = total.astype(BF)
            adj[at, k * BLOCK : (k + 1) * BLOCK] = high
            adj_lo[at, k * BLOCK : (k + 1) * BLOCK] = (total - high.astype(F32)).astype(BF)
        for k in range(NB, EXT):
            use = (rows[k] == i).astype(F32)
            adj[at, k * BLOCK : (k + 1) * BLOCK] = (tv[k].astype(F32) * use).astype(BF)
    hand_on(0, 0)
    for k in range(CHUNKS):
        adj_t[cols(k), :] = adj[:, cols(k)].T
    hand_on(0, 1)
    for j in range(CHUNKS):
        own_cells = ext[j, :CELL_DEV]
        msg[:, cols(j)] = dot(adj[:, :CELL_DEV], own_cells) + dot(adj_lo[...], own_cells)
    hand_on(0, 2)
    ids = pool[...]
    member = (ids == lax.broadcasted_iota(jnp.int32, (SN_DEV, CELL_DEV), 0)).astype(F32)
    member_b = member.astype(BF)
    wide = (ids == lax.broadcasted_iota(jnp.int32, (PAIR, CELL_DEV), 0)).astype(F32)
    member_t = wide.T.astype(BF)
    root = jnp.sqrt(jnp.sum(member, axis=1, keepdims=True))
    loads[1].wait()
    loads[2].wait()
    for j in range(CHUNKS):
        for k in range(CHUNKS):
            wm_t[cols(k), cols(j)] = wm[cols(j), cols(k)].T
            wq_t[cols(k), cols(j)] = wq[cols(j), cols(k)].T
    loads[3].wait()
    for j in range(CHUNKS):
        cv_t[cols(j), :] = cv[:, cols(j)].T

    for j in range(CHUNKS):
        for s in (2, 3):
            @pl.when(sides[s][0])
            def _():
                halo_recv(j, s).wait_recv()
        msg[:, cols(j)] += dot(adj[:, 2 * CELL_DEV :], ext[j, 2 * CELL_DEV :])
    for j in range(CHUNKS):
        for s in (0, 1):
            @pl.when(sides[s][0])
            def _():
                halo_recv(j, s).wait_recv()
        part = (
            msg[:, cols(j)]
            + dot(adj[:, CELL_DEV : 2 * CELL_DEV], ext[j, CELL_DEV : 2 * CELL_DEV])
        ).astype(BF)
        if j == CHUNKS - 1:
            break
        for k in range(CHUNKS):
            term = dot(part, wm[cols(j), cols(k)])
            hid[:, cols(k)] = term if j == 0 else hid[:, cols(k)] + term
    mine = pl.ds(pl.multiple_of(c * SN_DEV, SN_DEV), SN_DEV)
    for j in range(CHUNKS):
        hid[:, cols(j)] += dot(part, wm[cols(CHUNKS - 1), cols(j)])
        for first in range(0, CELL_DEV, 64):
            some = slice(first, first + 64)
            hidden = hid[some, cols(j)]
            sigma = jax.nn.sigmoid(hidden)
            sig[some, cols(j)] = sigma
            pas[some, cols(j)] = (ext[j, some].astype(F32) + hidden * sigma).astype(BF)
        passed = pas[:, cols(j)]
        keys[j, mine] = (dot(member_b, passed) / root).astype(BF)
        for off in range(1, n_blk):
            key_copy(j, off).start()
    for j in range(CHUNKS):
        qry[:, cols(j)] = dot(pas[...], wq[:, cols(j)]).astype(BF)

    lane = lax.broadcasted_iota(jnp.int32, (1, PAIR), 1)
    even_f = (lane < HEAD).astype(F32)
    even, odd = even_f.astype(BF), (1.0 - even_f).astype(BF)
    scale = HEAD ** (-0.5)
    line = lax.broadcasted_iota(jnp.int32, (PAIR, 1), 0)
    upper_f = (line < HEAD).astype(F32)
    upper, lower = upper_f.astype(BF), (1.0 - upper_f).astype(BF)
    per = CHUNK // PAIR
    for t in range(D // PAIR):
        at = cols(t, PAIR)
        group, inner = t // per, cols(t % per, PAIR)
        if t % per == 0:
            for off in range(1, n_blk):
                key_recv(group, off).wait_recv()
        kp = keys[group, :, inner]
        k2 = jnp.concatenate([kp * even, kp * odd], axis=0)
        kp_t = kp.T
        k2_t = jnp.concatenate([kp_t * upper, kp_t * lower], axis=1)
        qp, cp = qry[:, at], cv[:, at]
        w = t % 2
        sc[w] = dot_nt(k2, qp)
        sl[w] = dot(k2, cv_t[at, :])
        for h in range(2):
            head = slice(h * nk, (h + 1) * nk)
            for x in range(CELL_DEV // BLOCK):
                some = cols(x, BLOCK)
                scores = sc[w, head, some]
                top = jnp.max(scores, axis=0, keepdims=True)
                probs = jnp.exp2((scores - top) * (scale * LOG2E))
                probs = probs * (1.0 / jnp.sum(probs, axis=0, keepdims=True))
                rounded = probs.astype(BF)
                pb[w, head, some] = rounded
                slope = sl[w, head, some]
                centre = jnp.sum(rounded.astype(F32) * slope, axis=0, keepdims=True)
                ds[w, head, some] = (probs * (slope - centre) * scale).astype(BF)
        both = dot(ds[w], qp) + dot(pb[w], cp)
        kg[group, :, inner] = jnp.where(lane < HEAD, both[:nk], both[nk:]).astype(BF)
        if t % per == per - 1:
            for off in range(1, n_blk):
                part_copy(group, off).start()
        att[:, at] = dot(k2_t, pb[w]).astype(BF).T
        dqr[:, at] = dot(k2_t, ds[w]).astype(BF).T
    for j in range(CHUNKS):
        base[:, cols(j)] = cv[:, cols(j)].astype(F32) + dot(dqr[...], wq_t[:, cols(j)])
        sigma = sig[:, cols(j)]
        sig[:, cols(j)] = sigma * (1.0 + hid[:, cols(j)] * (1.0 - sigma))
    for j in range(CHUNKS):
        total = kg[j, mine].astype(F32)
        for off in range(1, n_blk):
            part_copy(j, off).wait_recv()
            total = total + kgr[j, off].astype(F32)
        spread = dot(member_t[:, :SN_DEV], (total / root).astype(BF))
        through = (base[:, cols(j)] + spread).astype(BF).astype(F32)
        base[:, cols(j)] = through
        dh[:, cols(j)] = (through * sig[:, cols(j)]).astype(BF)
    for j in range(CHUNKS):
        dmsg = dot(dh[...], wm_t[:, cols(j)]).astype(BF)
        dm[:, cols(j)] = dmsg
        back = dot(adj_t[CELL_DEV:, :], dmsg)
        for s in range(4):
            gs[j, s] = back[s * BLOCK : (s + 1) * BLOCK].astype(BF)
        if relay:
            for s in (0, 1):
                @pl.when(diagonal[s])
                def _():
                    to_middle(1, gs.at[j, s], ss, j, s).start()
        for s in range(4):
            @pl.when(straight(s))
            def _():
                grad_send(j, s).start()
    for j in range(CHUNKS):
        hand_on(1, j)
        own[:, cols(j)] = base[:, cols(j)] + dot(adj_t[:CELL_DEV, :], dm[:, cols(j)])
    for j in range(CHUNKS):
        for s in (2, 3, 0, 1):
            @pl.when(sides[s][0])
            def _():
                grad_recv(j, s).wait_recv()
        returned = (
            gr[j, 0].astype(F32) + gr[j, 1].astype(F32)
            + gr[j, 2].astype(F32) + gr[j, 3].astype(F32)
        )
        out[:BLOCK, cols(j)] = (own[:BLOCK, cols(j)] + returned * (1.0 - second)).astype(BF)
        out[BLOCK:, cols(j)] = (own[BLOCK:, cols(j)] + returned * second).astype(BF)

    for s in range(4):
        @pl.when(straight(s))
        def _():
            for j in range(CHUNKS):
                halo_send(j, s).wait_send()
                grad_send(j, s).wait_send()
    if relay:
        for s in (0, 1):
            @pl.when(diagonal[s])
            def _():
                for j in range(CHUNKS):
                    to_middle(0, bnd.at[j], hs, j, s).wait_send()
                    to_middle(1, gs.at[j, s], ss, j, s).wait_send()

            @pl.when(hands_on)
            def _():
                for j in range(CHUNKS):
                    from_middle(0, j, s).wait_send()
                    from_middle(1, j, s).wait_send()
    for off in range(1, n_blk):
        for j in range(CHUNKS):
            key_copy(j, off).wait_send()
            part_copy(j, off).wait_send()


def body(n_row, n_blk, cells, tile_rows, tile_cols, tile_count, halo_blocks, tile_vals, pool_ids,
         w_msg, w_query, cotangent):
    smem = pl.BlockSpec(memory_space=pltpu.SMEM)
    hbm = pl.BlockSpec(memory_space=pltpu.HBM)
    nk = SN_DEV * n_blk
    whole = (CELL_DEV, D)
    sem = pltpu.SemaphoreType.DMA
    return pl.pallas_call(
        functools.partial(kernel, n_row, n_blk),
        out_shape=[pltpu.VMEM(whole, BF)] * 3,
        in_specs=[hbm, hbm, hbm, smem, smem, hbm, hbm, hbm, hbm, hbm],
        out_specs=[pl.BlockSpec(memory_space=pltpu.VMEM)] * 3,
        scratch_shapes=[
            pltpu.VMEM((CHUNKS, EXT * BLOCK, CHUNK), BF),
            pltpu.VMEM((CHUNKS, BLOCK, CHUNK), BF),
            pltpu.VMEM((TILES, BLOCK, BLOCK), BF),
            pltpu.VMEM((D, D), BF),
            pltpu.VMEM((D, D), BF),
            pltpu.VMEM(whole, BF),
            pltpu.VMEM((CELL_DEV, EXT * BLOCK), BF),
            pltpu.VMEM((CELL_DEV, CELL_DEV), BF),
            pltpu.VMEM((EXT * BLOCK, CELL_DEV), BF),
            pltpu.VMEM((D, D), BF),
            pltpu.VMEM((D, D), BF),
            pltpu.VMEM(whole, F32),
            pltpu.VMEM(whole, F32),
            pltpu.VMEM(whole, F32),
            pltpu.VMEM(whole, BF),
            pltpu.VMEM((CHUNKS, nk, CHUNK), BF),
            pltpu.VMEM(whole, BF),
            pltpu.VMEM((CHUNKS, nk, CHUNK), BF),
            pltpu.VMEM((CHUNKS, n_blk, SN_DEV, CHUNK), BF),
            pltpu.VMEM((CHUNKS, 4, BLOCK, CHUNK), BF),
            pltpu.VMEM((CHUNKS, 4, BLOCK, CHUNK), BF),
            pltpu.VMEM(whole, F32),
            pltpu.VMEM(whole, BF),
            pltpu.VMEM(whole, F32),
            pltpu.VMEM(whole, BF),
            pltpu.VMEM((2, CHUNKS, 2, BLOCK, CHUNK), BF),
            pltpu.VMEM((D, CELL_DEV), BF),
            pltpu.VMEM((2, 2 * nk, CELL_DEV), F32),
            pltpu.VMEM((2, 2 * nk, CELL_DEV), F32),
            pltpu.VMEM((2, 2 * nk, CELL_DEV), BF),
            pltpu.VMEM((2, 2 * nk, CELL_DEV), BF),
            sem((CHUNKS,)), sem((5,)), sem((CHUNKS, 4)), sem((CHUNKS, 4)),
            sem((CHUNKS, n_blk)), sem((CHUNKS, n_blk)), sem((CHUNKS, n_blk)), sem((CHUNKS, n_blk)),
            sem((CHUNKS, 4)), sem((CHUNKS, 4)), sem((2, CHUNKS, 2)), sem((2, CHUNKS, 2)),
            pltpu.SMEM((TILES,), jnp.int32), pltpu.SMEM((TILES,), jnp.int32),
            pltpu.VMEM((1, CELL_DEV), jnp.int32), sem((3,)),
        ],
        compiler_params=pltpu.CompilerParams(
            collective_id=0, has_side_effects=True, vmem_limit_bytes=(62 * 1024 + 768) * 1024
        ),
    )(cells, tile_rows, tile_cols, tile_count, halo_blocks, tile_vals,
      pool_ids.reshape(1, CELL_DEV), w_msg, w_query, cotangent)


def solution(mesh):
    both = P(("row", "blk"))
    flat = P(("row", "blk"), None)
    return jax.shard_map(
        functools.partial(body, mesh.shape["row"], mesh.shape["blk"]),
        mesh=mesh,
        in_specs=(flat, both, both, both, both, P(("row", "blk"), None, None), both, P(), P(), flat),
        out_specs=(flat, flat, flat),
        check_vma=False,
    )
```
